256 devices in a mesh: samp: 8 (over y_lo, x), snp: 32 (over z, y_hi, core).
Axes of the slice: x: 4, y: 4 (y_hi: 2, y_lo: 2; y = y_hi * 2 + y_lo), z: 8, core: 2. Of those that a mesh axis runs over, the one named last changes fastest.
Arguments:
- genotypes: bfloat16 [2, 65536, 8192], P(None, 'samp', 'snp'), may hold values from 0 to 2, as said below
- ancestry: float32 [16, 65536], P(None, ('samp', 'snp')), may hold values from 0 to 1, as said below
- frequencies: float32 [2, 16, 8192], P(None, None, 'snp'), may hold values from 0.02 to 0.98
Outputs:
- new_frequencies: float32 [2, 16, 8192], P(None, None, 'snp')
- new_ancestry: float32 [16, 65536], P(None, ('samp', 'snp'))
The draws below stay inside these ranges and needn't reach their ends.
Inputs may be any that keep to these rules, and one draw needn't show every extreme that they name: `genotypes`: every entry is a whole count 0, 1 or 2. `ancestry`: all entries are positive and each sample's 16 proportions sum to 1.
All inputs are finite; a program needn't handle non-finite values.
Results may differ from the reference program's by a relative error of at most 0.0003.
Values sent between devices are 32-bit elements; how exact they have to be, the bound alone decides.
A program may use at most 128 MiB of HBM per device.

```python
import jax
import jax.numpy as jnp
from jax import lax

K = 16
ROWS = 8192
SLABS = 2
SAMPLES = 65536
SLAB = 8192
SNPS = 16384


def draw_ancestry(key, part):
    key = jax.random.fold_in(key, 7)
    spread = jnp.log(100.0)
    weights = jnp.exp(jax.random.uniform(key, (K, SAMPLES), jnp.float32, 0.0, 1.0) * spread)
    return (weights / jnp.sum(weights, axis=0, keepdims=True)).astype(jnp.float32)


def draw_genotypes(key, part):
    key = jax.random.fold_in(key, 11)
    counts = jax.random.randint(key, (SLABS, SAMPLES, SLAB), 0, 3, jnp.int32)
    return counts.astype(jnp.float32).astype(jnp.bfloat16)


def level_of(stream_key, shape, shards, low, largest):
    def one(axis_at, parts):
        heights = jax.random.uniform(jax.random.fold_in(jax.random.fold_in(stream_key, 6), axis_at), (parts,), jnp.float32, low / len(shards), largest / len(shards))
        return jnp.repeat(jnp.exp(heights), shape[axis_at] // parts).reshape((-1,) + (1,) * (len(shape) - axis_at - 1))

    factor_of = one(*shards[0])
    for cut in shards[1:]:
        factor_of = factor_of * one(*cut)
    return factor_of


def setup_inputs(seed: int = 0) -> dict:
    seeds = jax.random.split(jax.random.key(seed), 4)
    return {
        "genotypes": draw_genotypes(jax.random.fold_in(seeds[3], 71), 0),
        "ancestry": draw_ancestry(jax.random.fold_in(seeds[3], 71), 0),
        "frequencies": jnp.clip(0.02 + 0.96000002 * jax.random.uniform(seeds[2], (SLABS, K, SLAB), jnp.float32) ** level_of(seeds[2], (SLABS, K, SLAB), ((2, 32),), -0.2, 0.2), 0.02, 0.98),
    }


HIGH = lax.Precision.HIGHEST


def block_terms(counts, rows_q, freq_slab):
    allele_prob = lax.dot_general(rows_q, freq_slab, (((0,), (0,)), ((), ())), precision=HIGH, preferred_element_type=jnp.float32)
    values = counts.astype(jnp.float32)
    hit_ratio = values / allele_prob
    miss_ratio = (2.0 - values) / (1.0 - allele_prob)
    hit_sum = jnp.dot(rows_q, hit_ratio, precision=HIGH, preferred_element_type=jnp.float32)
    miss_sum = jnp.dot(rows_q, miss_ratio, precision=HIGH, preferred_element_type=jnp.float32)
    sample_share = lax.dot_general(freq_slab, hit_ratio, (((1,), (1,)), ((), ())), precision=HIGH, preferred_element_type=jnp.float32)
    sample_share = sample_share + lax.dot_general(1.0 - freq_slab, miss_ratio, (((1,), (1,)), ((), ())), precision=HIGH, preferred_element_type=jnp.float32)
    return hit_sum, miss_sum, sample_share


def reference(genotypes, ancestry, frequencies):
    block_count = SAMPLES // ROWS
    q_blocks = ancestry.reshape(K, block_count, ROWS).transpose(1, 0, 2)
    total_share = jnp.zeros((K, SAMPLES), jnp.float32)
    updated = []
    for slab_index in range(SLABS):
        freq_slab = frequencies[slab_index]
        g_blocks = genotypes[slab_index].reshape(block_count, ROWS, SLAB)
        hits, misses, shares = lax.map(lambda pair: block_terms(pair[0], pair[1], freq_slab), (g_blocks, q_blocks))
        hit_sum = jnp.sum(hits, axis=0)
        miss_sum = jnp.sum(misses, axis=0)
        weighted = freq_slab * hit_sum
        updated.append(weighted / (weighted + (1.0 - freq_slab) * miss_sum))
        total_share = total_share + shares.transpose(1, 0, 2).reshape(K, SAMPLES)
    new_ancestry = ancestry * total_share / (2.0 * SNPS)
    return jnp.stack(updated), new_ancestry
```

```python
import functools

import jax
import jax.numpy as jnp
from jax import lax
from jax.experimental import pallas as pl
from jax.experimental.pallas import tpu as pltpu
from jax.sharding import PartitionSpec as P

MESH = pl.DeviceIdType.MESH
bf16, f32 = jnp.bfloat16, jnp.float32

Z, YH, CORES, SAMP = 8, 2, 2, 8
BLOCK = 256
PLANE = YH * CORES * BLOCK


def split3(x):
    a = x.astype(bf16)
    r = x - a.astype(f32)
    b = r.astype(bf16)
    return a, b, (r - b.astype(f32)).astype(bf16)


def spread(shape, axis, step):
    t = lax.broadcasted_iota(jnp.int32, shape, axis).astype(f32) * step
    return t - jnp.floor(t)


S_STEP, C_STEP = 0.6180339887, 0.7548776662


def kernel(
    total,
    g_hbm, q_ref, f_ref, nf_ref, na_ref,
    g, qb, xd, xe, acc, qsum, rp, fw, scale, part, sib, inbox, ysum, ybuf,
    bsend, bin_, fp, nfp,
    g_sem, y_s, y_r, own_s, own_r, z_s, z_r, fwd_s, fwd_r, sib_s, sib_r,
    in_s, in_r, yo_s, yo_r, b_s, b_r, n_s, n_r,
):
    me = lax.axis_index("snp")
    a = lax.axis_index("samp")
    c = lax.rem(me, 2)
    yh = lax.rem(me // 2, 2)
    z = me // 4

    def snp_id(zz, yy, cc):
        return {"snp": zz * 4 + yy * 2 + cc}

    sibling = snp_id(z, yh, 1 - c)
    ymate = snp_id(z, 1 - yh, c)

    def plane(k):
        step = ((k + 1) // 2) * (2 * lax.rem(k, 2) - 1)
        return lax.rem(z + step + Z, Z)

    def remote(src, dst, ss, rs, dev):
        return pltpu.make_async_remote_copy(
            src_ref=src, dst_ref=dst, send_sem=ss, recv_sem=rs,
            device_id=dev, device_id_type=MESH,
        )

    def load_g(k):
        rows = pl.ds(pl.multiple_of(plane(k) * PLANE, PLANE), PLANE)
        return pltpu.make_async_copy(g_hbm.at[:, rows], g.at[:, rows], g_sem.at[k])

    bar = pltpu.get_barrier_semaphore()
    for dz in range(1, Z):
        pl.semaphore_signal(bar, inc=1, device_id=snp_id(lax.rem(z + dz, Z), yh, c), device_id_type=MESH)
    pl.semaphore_signal(bar, inc=1, device_id=sibling, device_id_type=MESH)
    pl.semaphore_signal(bar, inc=1, device_id=ymate, device_id_type=MESH)
    for da in range(1, SAMP):
        pl.semaphore_signal(bar, inc=1, device_id={"samp": lax.rem(a + da, SAMP)}, device_id_type=MESH)

    @pl.loop(0, Z)
    def _(k):
        load_g(k).start()

    qb[z, c, yh] = q_ref[...]
    pl.semaphore_wait(bar, Z + SAMP)

    own_q = qb.at[z, c, yh]
    to_sib = remote(own_q, own_q, own_s.at[0], own_r.at[0], sibling)
    to_y = remote(own_q, own_q, y_s, y_r, ymate)
    to_y.start()
    to_sib.start()

    inv_c = jnp.exp2(-spread((1, BLOCK), 1, C_STEP))
    inv_s = jnp.exp2(-spread((1, BLOCK), 1, S_STEP))
    scale[...] = jnp.exp2(spread((BLOCK, BLOCK), 0, S_STEP) + spread((BLOCK, BLOCK), 1, C_STEP))
    for s in range(2):
        f = f_ref[s]
        f0, f1, f2 = split3(2.0 * f)
        rp[s] = jnp.concatenate([f0, f1, f2, f0, f1, f0], axis=0)
        d0, d1, _ = split3(f * inv_c)
        fw[s] = jnp.concatenate([d0, d1], axis=0)
        for rg in range(2):
            for lh in range(2):
                fp[s * 4 + rg * 2 + lh] = f[rg * 8:rg * 8 + 8, lh * 128:lh * 128 + 128]
    acc[...] = jnp.zeros_like(acc)
    qsum[...] = jnp.zeros_like(qsum)
    xd[1] = jnp.zeros(xd.shape[1:], bf16)
    xe[1] = jnp.zeros(xe.shape[1:], bf16)

    def to_z(k):
        step = ((k + 1) // 2) * (2 * lax.rem(k, 2) - 1)
        zz = lax.rem(z - step + Z, Z)
        return remote(qb.at[z, c], qb.at[z, c], z_s.at[k], z_r.at[z], snp_id(zz, yh, c))

    def from_z(k):
        zz = plane(k)
        return remote(qb.at[zz, c], qb.at[zz, c], z_s.at[k], z_r.at[zz], snp_id(zz, yh, c))

    mate_q = qb.at[z, c, 1 - yh]
    remote(mate_q, mate_q, y_s, y_r, ymate).wait_recv()
    to_sib2 = remote(mate_q, mate_q, own_s.at[1], own_r.at[1], sibling)
    to_sib2.start()

    @pl.loop(1, Z)
    def _(k):
        to_z(k).start()

    for i in range(2):
        yy = yh if i == 0 else 1 - yh
        remote(
            qb.at[z, 1 - c, yy], qb.at[z, 1 - c, yy], own_s.at[i], own_r.at[i], sibling
        ).wait_recv()

    def fwd(k, core):
        zz = plane(k)
        return remote(qb.at[zz, core], qb.at[zz, core], fwd_s.at[k], fwd_r.at[k], sibling)

    def front(k, j, slot):
        zz = plane(k)
        q = qb[zz, j % 2, j // 2]
        q0, q1, q2 = split3(q)
        left = jnp.concatenate([q0, q0, q0, q1, q1, q2], axis=0)
        qsum[...] += q
        rows = pl.ds(pl.multiple_of(zz * PLANE + j * BLOCK, BLOCK), BLOCK)
        for s in range(2):
            p2 = lax.dot_general(left, rp[s], (((0,), (0,)), ((), ())), preferred_element_type=f32)
            u = 2.0 - p2
            r = pltpu.reciprocal(p2 * u, approx=True) * scale[...]
            d = (g[s, rows].astype(f32) - p2) * r
            xd[slot, s] = d.astype(bf16)
            xe[slot, s] = (u * d).astype(bf16)

    def back(k, j, slot):
        q0, q1, _ = split3(qb[plane(k), j % 2, j // 2] * inv_s)
        qq = jnp.concatenate([q0, q1], axis=0)
        share = None
        for s in range(2):
            d = xd[slot, s]
            acc[s, 0] += jnp.dot(qq, d, preferred_element_type=f32)
            acc[s, 1] += jnp.dot(qq, xe[slot, s], preferred_element_type=f32)
            o = lax.dot_general(fw[s], d, (((1,), (1,)), ((), ())), preferred_element_type=f32)
            share = o if share is None else share + o
        part[k, j % 2, j // 2] = share[:16] + share[16:]

    def sib_send(k):
        return remote(part.at[k, 1 - c], sib.at[k], sib_s.at[k], sib_r.at[k], sibling)

    def in_send(k):
        return remote(part.at[k, c], inbox.at[z], in_s.at[k], in_r.at[z], snp_id(plane(k), yh, c))

    def reduce_core(k):
        sib_send(k).wait_recv()
        part[k, c] = part[k, c] + sib[k]

    @pl.loop(0, Z)
    def _(k):
        @pl.when(k == 1)
        def _():
            from_z(k).wait_recv()
            fwd(k, c).start()

        @pl.when(jnp.logical_and(k >= 1, k < Z - 1))
        def _():
            from_z(k + 1).wait_recv()
            fwd(k + 1, c).start()

        @pl.when(k >= 1)
        def _():
            fwd(k, 1 - c).wait_recv()

        @pl.when(k >= 2)
        def _():
            sib_send(k - 2).start()

        @pl.when(k >= 3)
        def _():
            reduce_core(k - 3)

        @pl.when(k >= 4)
        def _():
            in_send(k - 3).start()

        load_g(k).wait()
        last = jnp.maximum(k - 1, 0)
        front(k, 0, 0)
        back(last, 3, 1)
        for j in range(1, 4):
            front(k, j, j % 2)
            back(k, j - 1, (j - 1) % 2)

    sib_send(Z - 2).start()
    back(Z - 1, 3, 1)
    sib_send(Z - 1).start()

    counts = jnp.sum(qsum[...], axis=1, keepdims=True)
    for s in range(2):
        diff = (acc[s, 0, :16] + acc[s, 0, 16:]) * (4.0 * inv_c)
        hit = (acc[s, 1, :16] + acc[s, 1, 16:]) * (2.0 * inv_c) + 2.0 * counts
        for rg in range(2):
            for lh in range(2):
                i = s * 4 + rg * 2 + lh
                bsend[i, 0] = hit[rg * 8:rg * 8 + 8, lh * 128:lh * 128 + 128]
                bsend[i, 1] = diff[rg * 8:rg * 8 + 8, lh * 128:lh * 128 + 128]

    def b_copy(da):
        to = lax.rem(a + da, SAMP)
        return remote(bsend.at[to], bin_.at[a], b_s.at[da], b_r.at[a], {"samp": to})

    def b_from(da):
        src = lax.rem(a + da, SAMP)
        return remote(bsend.at[a], bin_.at[src], b_s.at[da], b_r.at[src], {"samp": src})

    def n_copy(da):
        return remote(nfp.at[a], nfp.at[a], n_s.at[da], n_r.at[a], {"samp": lax.rem(a + da, SAMP)})

    def n_from(da):
        src = lax.rem(a + da, SAMP)
        return remote(nfp.at[src], nfp.at[src], n_s.at[da], n_r.at[src], {"samp": src})

    @pl.loop(1, SAMP)
    def _(da):
        b_copy(da).start()

    @pl.loop(Z - 3, Z)
    def _(k):
        reduce_core(k)
        in_send(k).start()

    @pl.loop(1, SAMP)
    def _(da):
        b_from(da).wait_recv()

    bin_[a] = bsend[a]
    both = jnp.sum(bin_[...], axis=0)
    f = fp[a]
    weighted = f * both[0]
    nfp[a] = weighted / (weighted + (1.0 - f) * (both[0] - both[1]))

    @pl.loop(1, SAMP)
    def _(da):
        n_copy(da).start()

    @pl.loop(1, Z)
    def _(k):
        zz = plane(k)
        remote(part.at[k, c], inbox.at[zz], in_s.at[k], in_r.at[zz], snp_id(zz, yh, c)).wait_recv()

    inbox[z] = part[0, c]
    ysum[...] = jnp.sum(inbox[...], axis=0)
    y_out = remote(ysum.at[1 - yh], ybuf, yo_s, yo_r, ymate)
    y_out.start()

    @pl.loop(1, SAMP)
    def _(da):
        n_from(da).wait_recv()

    for s in range(2):
        for rg in range(2):
            for lh in range(2):
                nf_ref[s, rg * 8:rg * 8 + 8, lh * 128:lh * 128 + 128] = nfp[s * 4 + rg * 2 + lh]

    y_out.wait_recv()
    q = q_ref[...]
    share = (ysum[yh] + ybuf[...]) * (4.0 * inv_s)
    rest = total - jnp.sum(q * share, axis=0, keepdims=True)
    na_ref[...] = q * (share + rest) * (1.0 / total)

    y_out.wait_send()
    to_y.wait_send()
    to_sib.wait_send()
    to_sib2.wait_send()

    @pl.loop(1, Z)
    def _(k):
        to_z(k).wait_send()
        fwd(k, c).wait_send()
        in_send(k).wait_send()
        b_copy(k).wait_send()
        n_copy(k).wait_send()

    @pl.loop(0, Z)
    def _(k):
        sib_send(k).wait_send()


def on_device(genotypes, ancestry, frequencies):
    slabs, rows, cols = genotypes.shape
    k = ancestry.shape[0]
    total = 2.0 * slabs * cols * lax.axis_size("snp")
    dma = pltpu.SemaphoreType.DMA
    vmem = pltpu.VMEM
    return pl.pallas_call(
        functools.partial(kernel, total),
        out_shape=(
            jax.ShapeDtypeStruct(frequencies.shape, f32),
            jax.ShapeDtypeStruct(ancestry.shape, f32),
        ),
        in_specs=[
            pl.BlockSpec(memory_space=pltpu.HBM),
            pl.BlockSpec(memory_space=vmem),
            pl.BlockSpec(memory_space=vmem),
        ],
        out_specs=(pl.BlockSpec(memory_space=vmem), pl.BlockSpec(memory_space=vmem)),
        scratch_shapes=[
            vmem(genotypes.shape, bf16),
            vmem((Z, CORES, YH, k, BLOCK), f32),
            vmem((2, slabs, BLOCK, cols), bf16),
            vmem((2, slabs, BLOCK, cols), bf16),
            vmem((slabs, 2, 2 * k, cols), f32),
            vmem((k, BLOCK), f32),
            vmem((slabs, 6 * k, cols), bf16),
            vmem((slabs, 2 * k, cols), bf16),
            vmem((BLOCK, cols), f32),
            vmem((Z, CORES, YH, k, BLOCK), f32),
            vmem((Z, YH, k, BLOCK), f32),
            vmem((Z, YH, k, BLOCK), f32),
            vmem((YH, k, BLOCK), f32),
            vmem((k, BLOCK), f32),
            vmem((SAMP, 2, 8, 128), f32),
            vmem((SAMP, 2, 8, 128), f32),
            vmem((SAMP, 8, 128), f32),
            vmem((SAMP, 8, 128), f32),
            dma((Z,)),
            dma(()), dma(()),
            dma((2,)), dma((2,)),
            dma((Z,)), dma((Z,)),
            dma((Z,)), dma((Z,)),
            dma((Z,)), dma((Z,)),
            dma((Z,)), dma((Z,)),
            dma(()), dma(()),
            dma((SAMP,)), dma((SAMP,)),
            dma((SAMP,)), dma((SAMP,)),
        ],
        compiler_params=pltpu.CompilerParams(
            collective_id=0, has_side_effects=True, vmem_limit_bytes=40 << 20
        ),
        name="em_step",
    )(genotypes, ancestry, frequencies)


def solution(mesh):
    in_specs = (P(None, "samp", "snp"), P(None, ("samp", "snp")), P(None, None, "snp"))
    out_specs = (P(None, None, "snp"), P(None, ("samp", "snp")))
    return jax.shard_map(
        on_device, mesh=mesh, in_specs=in_specs, out_specs=out_specs, check_vma=False
    )
```

```python
import functools

import jax
import jax.numpy as jnp
from jax import lax
from jax.experimental import pallas as pl
from jax.experimental.pallas import tpu as pltpu
from jax.sharding import PartitionSpec as P

MESH = pl.DeviceIdType.MESH
bf16, f32 = jnp.bfloat16, jnp.float32

Z, YH, CORES, SAMP = 8, 2, 2, 8
CHIPS = Z * YH
BLOCK = 256
PLANE = YH * CORES * BLOCK


def split3(x):
    a = x.astype(bf16)
    r = x - a.astype(f32)
    b = r.astype(bf16)
    return a, b, (r - b.astype(f32)).astype(bf16)


def spread(shape, axis, step):
    t = lax.broadcasted_iota(jnp.int32, shape, axis).astype(f32) * step
    return t - jnp.floor(t)


S_STEP, C_STEP = 0.6180339887, 0.7548776662


def kernel(
    total,
    g_hbm, q_hbm, f_hbm, nf_ref, na_ref,
    g, f_ref, qb, xd, xe, acc, qsum, rp, fw, scale, part, sib, inbox,
    bsend, bin_, fp, nfp,
    g_sem, qf_sem, q_s, q_r, fwd_s, fwd_r, sib_s, sib_r,
    in_s, in_r, b_s, b_r, n_s, n_r, column,
):
    me = lax.axis_index("snp")
    a = lax.axis_index("samp")
    c = lax.rem(me, 2)
    yh = lax.rem(me // 2, 2)
    z = me // 4

    def snp_id(zz, yy, cc):
        return {"snp": zz * 4 + yy * 2 + cc}

    sibling = snp_id(z, yh, 1 - c)

    def plane(k):
        step = ((k + 1) // 2) * (2 * lax.rem(k, 2) - 1)
        return lax.rem(z + step + Z, Z)

    def chip(n):
        return plane(lax.rem(n, Z)), lax.rem(yh + n // Z, 2)

    def remote(src, dst, ss, rs, dev):
        return pltpu.make_async_remote_copy(
            src_ref=src, dst_ref=dst, send_sem=ss, recv_sem=rs,
            device_id=dev, device_id_type=MESH,
        )

    def load_g(k):
        rows = pl.ds(pl.multiple_of(plane(k) * PLANE, PLANE), PLANE)
        return pltpu.make_async_copy(g_hbm.at[:, rows], g.at[:, rows], g_sem.at[k])

    bar = pltpu.get_barrier_semaphore()
    for n in range(1, Z + 1):
        zz, yy = chip(n)
        pl.semaphore_signal(bar, inc=1, device_id=snp_id(zz, yy, c), device_id_type=MESH)
    pl.semaphore_signal(bar, inc=1, device_id=sibling, device_id_type=MESH)
    for da in range(1, SAMP):
        pl.semaphore_signal(bar, inc=1, device_id={"samp": lax.rem(a + da, SAMP)}, device_id_type=MESH)

    q_in = pltpu.make_async_copy(q_hbm, qb.at[z, c, yh], qf_sem.at[0])
    f_in = pltpu.make_async_copy(f_hbm, f_ref, qf_sem.at[1])
    q_in.start()
    f_in.start()

    @pl.loop(0, Z)
    def _(k):
        load_g(k).start()

    inv_c = jnp.exp2(-spread((1, BLOCK), 1, C_STEP))
    inv_s = jnp.exp2(-spread((1, BLOCK), 1, S_STEP))
    scale[...] = jnp.exp2(spread((BLOCK, BLOCK), 0, S_STEP) + spread((BLOCK, BLOCK), 1, C_STEP))
    f_in.wait()
    for s in range(2):
        f = f_ref[s]
        f0, f1, f2 = split3(2.0 * f)
        rp[s] = jnp.concatenate([f0, f1, f2, f0, f1, f0], axis=0)
        d0, d1, _ = split3(f * inv_c)
        fw[s] = jnp.concatenate([d0, d1], axis=0)
        for rg in range(2):
            for lh in range(2):
                fp[s * 4 + rg * 2 + lh] = f[rg * 8:rg * 8 + 8, lh * 128:lh * 128 + 128]
    acc[...] = jnp.zeros_like(acc)
    qsum[...] = jnp.zeros_like(qsum)
    xd[1] = jnp.zeros(xd.shape[1:], bf16)
    xe[1] = jnp.zeros(xe.shape[1:], bf16)

    q_in.wait()
    pl.semaphore_wait(bar, Z + SAMP)
    pl.semaphore_signal(column, inc=1, device_id=snp_id(z, 1 - yh, c), device_id_type=MESH)

    def q_out(n):
        m = lax.rem(n, Z)
        step = ((m + 1) // 2) * (2 * lax.rem(m, 2) - 1)
        zz, yy = lax.rem(z - step + Z, Z), lax.rem(yh + n // Z, 2)
        here = qb.at[z, c, yh]
        return remote(here, here, q_s.at[n], q_r.at[n], snp_id(zz, yy, c))

    def q_in_from(n):
        zz, yy = chip(n)
        here = qb.at[zz, c, yy]
        return remote(here, here, q_s.at[n], q_r.at[n], snp_id(zz, yy, c))

    def fwd(n, core):
        zz, yy = chip(n)
        here = qb.at[zz, core, yy]
        return remote(here, here, fwd_s.at[n], fwd_r.at[n], sibling)

    fwd(0, c).start()

    @pl.loop(1, Z)
    def _(n):
        q_out(n).start()

    def front(n, j, slot):
        zz, yy = chip(n)
        q = qb[zz, j, yy]
        q0, q1, q2 = split3(q)
        left = jnp.concatenate([q0, q0, q0, q1, q1, q2], axis=0)
        qsum[...] += q
        rows = pl.ds(pl.multiple_of(zz * PLANE + yy * (2 * BLOCK) + j * BLOCK, BLOCK), BLOCK)
        for s in range(2):
            p2 = lax.dot_general(left, rp[s], (((0,), (0,)), ((), ())), preferred_element_type=f32)
            u = 2.0 - p2
            r = pltpu.reciprocal(p2 * u, approx=True) * scale[...]
            d = (g[s, rows].astype(f32) - p2) * r
            xd[slot, s] = d.astype(bf16)
            xe[slot, s] = (u * d).astype(bf16)

    def back(n, j, slot):
        zz, yy = chip(n)
        q0, q1, _ = split3(qb[zz, j, yy] * inv_s)
        qq = jnp.concatenate([q0, q1], axis=0)
        share = None
        for s in range(2):
            d = xd[slot, s]
            acc[s, 0] += jnp.dot(qq, d, preferred_element_type=f32)
            acc[s, 1] += jnp.dot(qq, xe[slot, s], preferred_element_type=f32)
            o = lax.dot_general(fw[s], d, (((1,), (1,)), ((), ())), preferred_element_type=f32)
            share = o if share is None else share + o
        part[j, n] = share[:16] + share[16:]

    def sib_send(k):
        pair = pl.ds(2 * k, 2)
        return remote(part.at[1 - c, pair], sib.at[pair], sib_s.at[k], sib_r.at[k], sibling)

    def in_send(n):
        zz, yy = chip(n)
        return remote(part.at[c, n], inbox.at[n], in_s.at[n], in_r.at[n], snp_id(zz, yy, c))

    def reduce_core(k):
        sib_send(k).wait_recv()
        pair = pl.ds(2 * k, 2)
        part[c, pair] = part[c, pair] + sib[pair]

    fwd(0, 1 - c).wait_recv()
    load_g(0).wait()
    front(0, 0, 0)
    front(0, 1, 1)
    back(0, 0, 0)
    pl.semaphore_wait(column, 1)

    @pl.loop(Z, CHIPS)
    def _(n):
        q_out(n).start()

    for n in range(1, 3):
        q_in_from(n).wait_recv()
        fwd(n, c).start()

    @pl.loop(0, Z - 1)
    def _(k):
        q_in_from(2 * k + 3).wait_recv()
        fwd(2 * k + 3, c).start()

        @pl.when(k < Z - 2)
        def _():
            q_in_from(2 * k + 4).wait_recv()
            fwd(2 * k + 4, c).start()

        @pl.when(k >= 1)
        def _():
            sib_send(k - 1).start()

        @pl.when(k >= 2)
        def _():
            reduce_core(k - 2)
            in_send(2 * k - 3).start()

        @pl.when(k >= 3)
        def _():
            in_send(2 * k - 4).start()

        fwd(2 * k + 1, 1 - c).wait_recv()
        fwd(2 * k + 2, 1 - c).wait_recv()

        @pl.when(k < Z // 2)
        def _():
            load_g(2 * k + 1).wait()

        @pl.when(k < Z // 2 - 1)
        def _():
            load_g(2 * k + 2).wait()

        front(2 * k + 1, 0, 0)
        back(2 * k, 1, 1)
        front(2 * k + 1, 1, 1)
        back(2 * k + 1, 0, 0)
        front(2 * k + 2, 0, 0)
        back(2 * k + 1, 1, 1)
        front(2 * k + 2, 1, 1)
        back(2 * k + 2, 0, 0)

    sib_send(Z - 2).start()
    reduce_core(Z - 3)
    in_send(2 * Z - 6).start()
    in_send(2 * Z - 5).start()
    last = CHIPS - 1
    fwd(last, 1 - c).wait_recv()
    front(last, 0, 0)
    back(last - 1, 1, 1)
    front(last, 1, 1)
    back(last, 0, 0)
    back(last, 1, 1)
    sib_send(Z - 1).start()

    counts = jnp.sum(qsum[...], axis=1, keepdims=True)
    for s in range(2):
        diff = (acc[s, 0, :16] + acc[s, 0, 16:]) * (4.0 * inv_c)
        hit = (acc[s, 1, :16] + acc[s, 1, 16:]) * (2.0 * inv_c) + 2.0 * counts
        for rg in range(2):
            for lh in range(2):
                i = s * 4 + rg * 2 + lh
                bsend[i, 0] = hit[rg * 8:rg * 8 + 8, lh * 128:lh * 128 + 128]
                bsend[i, 1] = diff[rg * 8:rg * 8 + 8, lh * 128:lh * 128 + 128]

    def b_copy(da):
        to = lax.rem(a + da, SAMP)
        return remote(bsend.at[to], bin_.at[a], b_s.at[da], b_r.at[a], {"samp": to})

    def b_from(da):
        src = lax.rem(a + da, SAMP)
        return remote(bsend.at[a], bin_.at[src], b_s.at[da], b_r.at[src], {"samp": src})

    def n_copy(da):
        return remote(nfp.at[a], nfp.at[a], n_s.at[da], n_r.at[a], {"samp": lax.rem(a + da, SAMP)})

    def n_from(da):
        src = lax.rem(a + da, SAMP)
        return remote(nfp.at[src], nfp.at[src], n_s.at[da], n_r.at[src], {"samp": src})

    @pl.loop(1, SAMP)
    def _(da):
        b_copy(da).start()

    for k in range(Z - 2, Z):
        reduce_core(k)
        in_send(2 * k).start()
        in_send(2 * k + 1).start()

    @pl.loop(1, SAMP)
    def _(da):
        b_from(da).wait_recv()

    bin_[a] = bsend[a]
    both = jnp.sum(bin_[...], axis=0)
    f = fp[a]
    weighted = f * both[0]
    nfp[a] = weighted / (weighted + (1.0 - f) * (both[0] - both[1]))

    @pl.loop(1, SAMP)
    def _(da):
        n_copy(da).start()

    @pl.loop(1, CHIPS)
    def _(n):
        remote(part.at[c, n], inbox.at[n], in_s.at[n], in_r.at[n], sibling).wait_recv()

    inbox[0] = part[c, 0]

    @pl.loop(1, SAMP)
    def _(da):
        n_from(da).wait_recv()

    for s in range(2):
        for rg in range(2):
            for lh in range(2):
                nf_ref[s, rg * 8:rg * 8 + 8, lh * 128:lh * 128 + 128] = nfp[s * 4 + rg * 2 + lh]

    q = qb[z, c, yh]
    share = jnp.sum(inbox[...], axis=0) * (4.0 * inv_s)
    rest = total - jnp.sum(q * share, axis=0, keepdims=True)
    na_ref[...] = q * (share + rest) * (1.0 / total)

    @pl.loop(0, CHIPS)
    def _(n):
        fwd(n, c).wait_send()

    @pl.loop(1, CHIPS)
    def _(n):
        q_out(n).wait_send()
        in_send(n).wait_send()

    @pl.loop(0, Z)
    def _(k):
        sib_send(k).wait_send()

    @pl.loop(1, SAMP)
    def _(da):
        b_copy(da).wait_send()
        n_copy(da).wait_send()


def on_device(genotypes, ancestry, frequencies):
    slabs, rows, cols = genotypes.shape
    k = ancestry.shape[0]
    total = 2.0 * slabs * cols * lax.axis_size("snp")
    dma = pltpu.SemaphoreType.DMA
    vmem = pltpu.VMEM
    return pl.pallas_call(
        functools.partial(kernel, total),
        out_shape=(
            jax.ShapeDtypeStruct(frequencies.shape, f32),
            jax.ShapeDtypeStruct(ancestry.shape, f32),
        ),
        in_specs=[
            pl.BlockSpec(memory_space=pltpu.HBM),
            pl.BlockSpec(memory_space=pltpu.HBM),
            pl.BlockSpec(memory_space=pltpu.HBM),
        ],
        out_specs=(pl.BlockSpec(memory_space=vmem), pl.BlockSpec(memory_space=vmem)),
        scratch_shapes=[
            vmem(genotypes.shape, bf16),
            vmem(frequencies.shape, f32),
            vmem((Z, CORES, YH, k, BLOCK), f32),
            vmem((2, slabs, BLOCK, cols), bf16),
            vmem((2, slabs, BLOCK, cols), bf16),
            vmem((slabs, 2, 2 * k, cols), f32),
            vmem((k, BLOCK), f32),
            vmem((slabs, 6 * k, cols), bf16),
            vmem((slabs, 2 * k, cols), bf16),
            vmem((BLOCK, cols), f32),
            vmem((CORES, CHIPS, k, BLOCK), f32),
            vmem((CHIPS, k, BLOCK), f32),
            vmem((CHIPS, k, BLOCK), f32),
            vmem((SAMP, 2, 8, 128), f32),
            vmem((SAMP, 2, 8, 128), f32),
            vmem((SAMP, 8, 128), f32),
            vmem((SAMP, 8, 128), f32),
            dma((Z,)), dma((2,)),
            dma((CHIPS,)), dma((CHIPS,)),
            dma((CHIPS,)), dma((CHIPS,)),
            dma((Z,)), dma((Z,)),
            dma((CHIPS,)), dma((CHIPS,)),
            dma((SAMP,)), dma((SAMP,)),
            dma((SAMP,)), dma((SAMP,)),
            pltpu.SemaphoreType.REGULAR,
        ],
        compiler_params=pltpu.CompilerParams(
            collective_id=0, has_side_effects=True, vmem_limit_bytes=64 << 20
        ),
        name="em_step",
    )(genotypes, ancestry, frequencies)


def solution(mesh):
    in_specs = (P(None, "samp", "snp"), P(None, ("samp", "snp")), P(None, None, "snp"))
    out_specs = (P(None, None, "snp"), P(None, ("samp", "snp")))
    return jax.shard_map(
        on_device, mesh=mesh, in_specs=in_specs, out_specs=out_specs, check_vma=False
    )
```

```python
import functools

import jax
import jax.numpy as jnp
from jax import lax
from jax.experimental import pallas as pl
from jax.experimental.pallas import tpu as pltpu
from jax.sharding import PartitionSpec as P

MESH = pl.DeviceIdType.MESH
bf16, f32 = jnp.bfloat16, jnp.float32

Z, YH, CORES, SAMP = 8, 2, 2, 8
CHIPS = Z * YH
BLOCK = 256
PLANE = YH * CORES * BLOCK


def split3(x):
    a = x.astype(bf16)
    r = x - a.astype(f32)
    b = r.astype(bf16)
    return a, b, (r - b.astype(f32)).astype(bf16)


def spread(shape, axis, step):
    t = lax.broadcasted_iota(jnp.int32, shape, axis).astype(f32) * step
    return t - jnp.floor(t)


S_STEP, C_STEP = 0.6180339887, 0.7548776662


def kernel(
    total,
    g_hbm, q_hbm, f_hbm, nf_ref, na_ref,
    g, f_ref, qb, xd, xe, acc, qsum, rp, fw, scale, part, sib, inbox,
    bsend, bin_, fp, nfp,
    g_sem, qf_sem, q_s, q_r, fwd_s, fwd_r, sib_s, sib_r,
    in_s, in_r, b_s, b_r, n_s, n_r, column,
):
    me = lax.axis_index("snp")
    a = lax.axis_index("samp")
    c = lax.rem(me, 2)
    yh = lax.rem(me // 2, 2)
    z = me // 4

    def snp_id(zz, yy, cc):
        return {"snp": zz * 4 + yy * 2 + cc}

    sibling = snp_id(z, yh, 1 - c)

    def plane(k):
        step = ((k + 1) // 2) * (2 * lax.rem(k, 2) - 1)
        return lax.rem(z + step + Z, Z)

    def chip(n):
        return plane(lax.rem(n, Z)), lax.rem(yh + n // Z, 2)

    def remote(src, dst, ss, rs, dev):
        return pltpu.make_async_remote_copy(
            src_ref=src, dst_ref=dst, send_sem=ss, recv_sem=rs,
            device_id=dev, device_id_type=MESH,
        )

    def load_g(k):
        rows = pl.ds(pl.multiple_of(plane(k) * PLANE, PLANE), PLANE)
        return pltpu.make_async_copy(g_hbm.at[:, rows], g.at[:, rows], g_sem.at[k])

    bar = pltpu.get_barrier_semaphore()
    for n in range(1, Z + 1):
        zz, yy = chip(n)
        pl.semaphore_signal(bar, inc=1, device_id=snp_id(zz, yy, c), device_id_type=MESH)
    pl.semaphore_signal(bar, inc=1, device_id=sibling, device_id_type=MESH)
    for da in range(1, SAMP):
        pl.semaphore_signal(bar, inc=1, device_id={"samp": lax.rem(a + da, SAMP)}, device_id_type=MESH)

    q_in = pltpu.make_async_copy(q_hbm, qb.at[z, c, yh], qf_sem.at[0])
    f_in = pltpu.make_async_copy(f_hbm, f_ref, qf_sem.at[1])
    q_in.start()
    f_in.start()

    @pl.loop(0, Z)
    def _(k):
        load_g(k).start()

    inv_c = jnp.exp2(-spread((1, BLOCK), 1, C_STEP))
    inv_s = jnp.exp2(-spread((1, BLOCK), 1, S_STEP))
    scale[...] = jnp.exp2(spread((BLOCK, BLOCK), 0, S_STEP) + spread((BLOCK, BLOCK), 1, C_STEP))
    f_in.wait()
    for s in range(2):
        f = f_ref[s]
        f0, f1, f2 = split3(2.0 * f)
        rp[s] = jnp.concatenate([f0, f1, f2, f0, f1, f0], axis=0)
        d0, d1, _ = split3(f * inv_c)
        fw[s] = jnp.concatenate([d0, d1], axis=0)
        for rg in range(2):
            for lh in range(2):
                fp[s * 4 + rg * 2 + lh] = f[rg * 8:rg * 8 + 8, lh * 128:lh * 128 + 128]
    acc[...] = jnp.zeros_like(acc)
    qsum[...] = jnp.zeros_like(qsum)
    xd[1] = jnp.zeros(xd.shape[1:], bf16)
    xe[1] = jnp.zeros(xe.shape[1:], bf16)

    q_in.wait()
    pl.semaphore_wait(bar, Z + SAMP)
    pl.semaphore_signal(column, inc=1, device_id=snp_id(z, 1 - yh, c), device_id_type=MESH)

    def q_out(n):
        m = lax.rem(n, Z)
        step = ((m + 1) // 2) * (2 * lax.rem(m, 2) - 1)
        zz, yy = lax.rem(z - step + Z, Z), lax.rem(yh + n // Z, 2)
        here = qb.at[z, c, yh]
        return remote(here, here, q_s.at[n], q_r.at[n], snp_id(zz, yy, c))

    def q_in_from(n):
        zz, yy = chip(n)
        here = qb.at[zz, c, yy]
        return remote(here, here, q_s.at[n], q_r.at[n], snp_id(zz, yy, c))

    def fwd(n, core):
        zz, yy = chip(n)
        here = qb.at[zz, core, yy]
        return remote(here, here, fwd_s.at[n], fwd_r.at[n], sibling)

    fwd(0, c).start()

    @pl.loop(1, Z)
    def _(n):
        q_out(n).start()

    def front(n, j, slot):
        zz, yy = chip(n)
        q = qb[zz, j, yy]
        q0, q1, q2 = split3(q)
        left = jnp.concatenate([q0, q0, q0, q1, q1, q2], axis=0)
        qsum[...] += q
        rows = pl.ds(pl.multiple_of(zz * PLANE + yy * (2 * BLOCK) + j * BLOCK, BLOCK), BLOCK)
        for s in range(2):
            p2 = lax.dot_general(left, rp[s], (((0,), (0,)), ((), ())), preferred_element_type=f32)
            u = 2.0 - p2
            r = pltpu.reciprocal(p2 * u, approx=True) * scale[...]
            d = (g[s, rows].astype(f32) - p2) * r
            xd[slot, s] = d.astype(bf16)
            xe[slot, s] = (u * d).astype(bf16)

    def back(n, j, slot):
        zz, yy = chip(n)
        q0, q1, _ = split3(qb[zz, j, yy] * inv_s)
        qq = jnp.concatenate([q0, q1], axis=0)
        share = None
        for s in range(2):
            d = xd[slot, s]
            acc[s, 0] += jnp.dot(qq, d, preferred_element_type=f32)
            acc[s, 1] += jnp.dot(qq, xe[slot, s], preferred_element_type=f32)
            o = lax.dot_general(fw[s], d, (((1,), (1,)), ((), ())), preferred_element_type=f32)
            share = o if share is None else share + o
        part[j, n] = share[:16] + share[16:]

    def sib_send(k):
        pair = pl.ds(2 * k, 2)
        return remote(part.at[1 - c, pair], sib.at[pair], sib_s.at[k], sib_r.at[k], sibling)

    def in_send(n):
        zz, yy = chip(n)
        return remote(part.at[c, n], inbox.at[n], in_s.at[n], in_r.at[n], snp_id(zz, yy, c))

    def reduce_core(k):
        sib_send(k).wait_recv()
        pair = pl.ds(2 * k, 2)
        part[c, pair] = part[c, pair] + sib[pair]

    fwd(0, 1 - c).wait_recv()
    load_g(0).wait()
    front(0, 0, 0)
    front(0, 1, 1)
    back(0, 0, 0)
    pl.semaphore_wait(column, 1)

    @pl.loop(Z, CHIPS)
    def _(n):
        q_out(n).start()

    for n in range(1, 3):
        q_in_from(n).wait_recv()
        fwd(n, c).start()

    @pl.loop(0, Z - 1)
    def _(k):
        q_in_from(2 * k + 3).wait_recv()
        fwd(2 * k + 3, c).start()

        @pl.when(k < Z - 2)
        def _():
            q_in_from(2 * k + 4).wait_recv()
            fwd(2 * k + 4, c).start()

        @pl.when(k >= 1)
        def _():
            sib_send(k - 1).start()

        @pl.when(k >= 2)
        def _():
            reduce_core(k - 2)
            in_send(2 * k - 3).start()

        @pl.when(k >= 3)
        def _():
            in_send(2 * k - 4).start()

        fwd(2 * k + 1, 1 - c).wait_recv()
        fwd(2 * k + 2, 1 - c).wait_recv()

        @pl.when(k < Z // 2)
        def _():
            load_g(2 * k + 1).wait()

        @pl.when(k < Z // 2 - 1)
        def _():
            load_g(2 * k + 2).wait()

        front(2 * k + 1, 0, 0)
        back(2 * k, 1, 1)
        front(2 * k + 1, 1, 1)
        back(2 * k + 1, 0, 0)
        front(2 * k + 2, 0, 0)
        back(2 * k + 1, 1, 1)
        front(2 * k + 2, 1, 1)
        back(2 * k + 2, 0, 0)

    sib_send(Z - 2).start()
    reduce_core(Z - 3)
    in_send(2 * Z - 6).start()
    in_send(2 * Z - 5).start()
    last = CHIPS - 1
    fwd(last, 1 - c).wait_recv()
    front(last, 0, 0)
    back(last - 1, 1, 1)
    front(last, 1, 1)
    back(last, 0, 0)
    back(last, 1, 1)
    sib_send(Z - 1).start()

    counts = jnp.sum(qsum[...], axis=1, keepdims=True)
    for s in range(2):
        diff = (acc[s, 0, :16] + acc[s, 0, 16:]) * (4.0 * inv_c)
        hit = (acc[s, 1, :16] + acc[s, 1, 16:]) * (2.0 * inv_c) + 2.0 * counts
        for rg in range(2):
            for lh in range(2):
                i = s * 4 + rg * 2 + lh
                bsend[i, 0] = hit[rg * 8:rg * 8 + 8, lh * 128:lh * 128 + 128]
                bsend[i, 1] = diff[rg * 8:rg * 8 + 8, lh * 128:lh * 128 + 128]

    def b_copy(da):
        to = lax.rem(a + da, SAMP)
        return remote(bsend.at[to], bin_.at[a], b_s.at[da], b_r.at[a], {"samp": to})

    def b_from(da):
        src = lax.rem(a + da, SAMP)
        return remote(bsend.at[a], bin_.at[src], b_s.at[da], b_r.at[src], {"samp": src})

    def n_copy(da):
        return remote(nfp.at[a], nfp.at[a], n_s.at[da], n_r.at[a], {"samp": lax.rem(a + da, SAMP)})

    def n_from(da):
        src = lax.rem(a + da, SAMP)
        return remote(nfp.at[src], nfp.at[src], n_s.at[da], n_r.at[src], {"samp": src})

    @pl.loop(1, SAMP)
    def _(da):
        b_copy(da).start()

    for k in range(Z - 2, Z):
        reduce_core(k)
        in_send(2 * k).start()
        in_send(2 * k + 1).start()

    @pl.loop(1, SAMP)
    def _(da):
        b_from(da).wait_recv()

    bin_[a] = bsend[a]
    both = jnp.sum(bin_[...], axis=0)
    f = fp[a]
    weighted = f * both[0]
    nfp[a] = weighted / (weighted + (1.0 - f) * (both[0] - both[1]))

    @pl.loop(1, SAMP)
    def _(da):
        n_copy(da).start()

    @pl.loop(1, CHIPS)
    def _(n):
        remote(part.at[c, n], inbox.at[n], in_s.at[n], in_r.at[n], sibling).wait_recv()

    inbox[0] = part[c, 0]

    @pl.loop(1, SAMP)
    def _(da):
        n_from(da).wait_recv()

    for s in range(2):
        for rg in range(2):
            for lh in range(2):
                nf_ref[s, rg * 8:rg * 8 + 8, lh * 128:lh * 128 + 128] = nfp[s * 4 + rg * 2 + lh]

    q = qb[z, c, yh]
    share = jnp.sum(inbox[...], axis=0) * (4.0 * inv_s)
    rest = total - jnp.sum(q * share, axis=0, keepdims=True)
    na_ref[...] = q * (share + rest) * (1.0 / total)

    @pl.loop(0, CHIPS)
    def _(n):
        fwd(n, c).wait_send()

    @pl.loop(1, CHIPS)
    def _(n):
        q_out(n).wait_send()
        in_send(n).wait_send()

    @pl.loop(0, Z)
    def _(k):
        sib_send(k).wait_send()

    @pl.loop(1, SAMP)
    def _(da):
        b_copy(da).wait_send()
        n_copy(da).wait_send()


def on_device(genotypes, ancestry, frequencies):
    slabs, rows, cols = genotypes.shape
    k = ancestry.shape[0]
    total = 2.0 * slabs * cols * lax.axis_size("snp")
    dma = pltpu.SemaphoreType.DMA
    vmem = pltpu.VMEM
    return pl.pallas_call(
        functools.partial(kernel, total),
        out_shape=(
            jax.ShapeDtypeStruct(frequencies.shape, f32),
            jax.ShapeDtypeStruct(ancestry.shape, f32),
        ),
        in_specs=[
            pl.BlockSpec(memory_space=pltpu.HBM),
            pl.BlockSpec(memory_space=pltpu.HBM),
            pl.BlockSpec(memory_space=pltpu.HBM),
        ],
        out_specs=(pl.BlockSpec(memory_space=vmem), pl.BlockSpec(memory_space=vmem)),
        scratch_shapes=[
            vmem(genotypes.shape, bf16),
            vmem(frequencies.shape, f32),
            vmem((Z, CORES, YH, k, BLOCK), f32),
            vmem((2, slabs, BLOCK, cols), bf16),
            vmem((2, slabs, BLOCK, cols), bf16),
            vmem((slabs, 2, 2 * k, cols), f32),
            vmem((k, BLOCK), f32),
            vmem((slabs, 6 * k, cols), bf16),
            vmem((slabs, 2 * k, cols), bf16),
            vmem((BLOCK, cols), f32),
            vmem((CORES, CHIPS, k, BLOCK), f32),
            vmem((CHIPS, k, BLOCK), f32),
            vmem((CHIPS, k, BLOCK), f32),
            vmem((SAMP, 2, 8, 128), f32),
            vmem((SAMP, 2, 8, 128), f32),
            vmem((SAMP, 8, 128), f32),
            vmem((SAMP, 8, 128), f32),
            dma((Z,)), dma((2,)),
            dma((CHIPS,)), dma((CHIPS,)),
            dma((CHIPS,)), dma((CHIPS,)),
            dma((Z,)), dma((Z,)),
            dma((CHIPS,)), dma((CHIPS,)),
            dma((SAMP,)), dma((SAMP,)),
            dma((SAMP,)), dma((SAMP,)),
            pltpu.SemaphoreType.REGULAR,
        ],
        compiler_params=pltpu.CompilerParams(
            collective_id=0, has_side_effects=True, vmem_limit_bytes=55212 << 10
        ),
        name="em_step",
    )(genotypes, ancestry, frequencies)


def solution(mesh):
    in_specs = (P(None, "samp", "snp"), P(None, ("samp", "snp")), P(None, None, "snp"))
    out_specs = (P(None, None, "snp"), P(None, ("samp", "snp")))
    return jax.shard_map(
        on_device, mesh=mesh, in_specs=in_specs, out_specs=out_specs, check_vma=False
    )
```

```python
import functools

import jax
import jax.numpy as jnp
from jax import lax
from jax.experimental import pallas as pl
from jax.experimental.pallas import tpu as pltpu
from jax.sharding import PartitionSpec as P

MESH = pl.DeviceIdType.MESH
bf16, f32 = jnp.bfloat16, jnp.float32

Z, YH, CORES, SAMP = 8, 2, 2, 8
CHIPS = Z * YH
BLOCK = 256
PLANE = YH * CORES * BLOCK


def split3(x):
    a = x.astype(bf16)
    r = x - a.astype(f32)
    b = r.astype(bf16)
    return a, b, (r - b.astype(f32)).astype(bf16)


def spread(shape, axis, step):
    t = lax.broadcasted_iota(jnp.int32, shape, axis).astype(f32) * step
    return t - jnp.floor(t)


S_STEP, C_STEP = 0.6180339887, 0.7548776662


def kernel(
    total,
    g_hbm, q_hbm, f_hbm, nf_ref, na_ref,
    g, f_ref, qb, xd, xe, acc, qsum, rp, fw, scale, part, sib, inbox,
    bsend, bin_, fp, nfp,
    g_sem, qf_sem, q_s, q_r, fwd_s, fwd_r, sib_s, sib_r,
    in_s, in_r, b_s, b_r, n_s, n_r, column,
):
    me = lax.axis_index("snp")
    a = lax.axis_index("samp")
    c = lax.rem(me, 2)
    yh = lax.rem(me // 2, 2)
    z = me // 4

    def snp_id(zz, yy, cc):
        return {"snp": zz * 4 + yy * 2 + cc}

    sibling = snp_id(z, yh, 1 - c)

    def plane(k):
        step = ((k + 1) // 2) * (2 * lax.rem(k, 2) - 1)
        return lax.rem(z + step + Z, Z)

    def chip(n):
        return plane(lax.rem(n, Z)), lax.rem(yh + n // Z, 2)

    def remote(src, dst, ss, rs, dev):
        return pltpu.make_async_remote_copy(
            src_ref=src, dst_ref=dst, send_sem=ss, recv_sem=rs,
            device_id=dev, device_id_type=MESH,
        )

    def load_g(k):
        rows = pl.ds(pl.multiple_of(plane(k) * PLANE, PLANE), PLANE)
        return pltpu.make_async_copy(g_hbm.at[:, rows], g.at[:, rows], g_sem.at[k])

    bar = pltpu.get_barrier_semaphore()
    for n in range(1, Z + 1):
        zz, yy = chip(n)
        pl.semaphore_signal(bar, inc=1, device_id=snp_id(zz, yy, c), device_id_type=MESH)
    pl.semaphore_signal(bar, inc=1, device_id=sibling, device_id_type=MESH)
    for da in range(1, SAMP):
        pl.semaphore_signal(bar, inc=1, device_id={"samp": lax.rem(a + da, SAMP)}, device_id_type=MESH)

    q_in = pltpu.make_async_copy(q_hbm, qb.at[z, c, yh], qf_sem.at[0])
    f_in = pltpu.make_async_copy(f_hbm, f_ref, qf_sem.at[1])
    q_in.start()
    f_in.start()

    @pl.loop(0, Z)
    def _(k):
        load_g(k).start()

    inv_c = jnp.exp2(-spread((1, BLOCK), 1, C_STEP))
    inv_s = jnp.exp2(-spread((1, BLOCK), 1, S_STEP))
    scale[...] = jnp.exp2(spread((BLOCK, BLOCK), 0, S_STEP) + spread((BLOCK, BLOCK), 1, C_STEP))
    f_in.wait()
    for s in range(2):
        f = f_ref[s]
        f0, f1, f2 = split3(2.0 * f)
        rp[s] = jnp.concatenate([f0, f1, f2, f0, f1, f0], axis=0)
        d0, d1, _ = split3(f * inv_c)
        fw[s] = jnp.concatenate([d0, d1], axis=0)
        for rg in range(2):
            for lh in range(2):
                fp[s * 4 + rg * 2 + lh] = f[rg * 8:rg * 8 + 8, lh * 128:lh * 128 + 128]
    acc[...] = jnp.zeros_like(acc)
    qsum[...] = jnp.zeros_like(qsum)
    xd[1] = jnp.zeros(xd.shape[1:], bf16)
    xe[1] = jnp.zeros(xe.shape[1:], bf16)

    q_in.wait()
    pl.semaphore_wait(bar, Z + SAMP)
    pl.semaphore_signal(column, inc=1, device_id=snp_id(z, 1 - yh, c), device_id_type=MESH)

    def q_out(n):
        m = lax.rem(n, Z)
        step = ((m + 1) // 2) * (2 * lax.rem(m, 2) - 1)
        zz, yy = lax.rem(z - step + Z, Z), lax.rem(yh + n // Z, 2)
        here = qb.at[z, c, yh]
        return remote(here, here, q_s.at[n], q_r.at[n], snp_id(zz, yy, c))

    def q_in_from(n):
        zz, yy = chip(n)
        here = qb.at[zz, c, yy]
        return remote(here, here, q_s.at[n], q_r.at[n], snp_id(zz, yy, c))

    def fwd(n, core):
        zz, yy = chip(n)
        here = qb.at[zz, core, yy]
        return remote(here, here, fwd_s.at[n], fwd_r.at[n], sibling)

    fwd(0, c).start()

    @pl.loop(1, Z)
    def _(n):
        q_out(n).start()

    def front(n, j, slot):
        zz, yy = chip(n)
        q = qb[zz, j, yy]
        q0, q1, q2 = split3(q)
        left = jnp.concatenate([q0, q0, q0, q1, q1, q2], axis=0)
        qsum[...] += q
        rows = pl.ds(pl.multiple_of(zz * PLANE + yy * (2 * BLOCK) + j * BLOCK, BLOCK), BLOCK)
        for s in range(2):
            p2 = lax.dot_general(left, rp[s], (((0,), (0,)), ((), ())), preferred_element_type=f32)
            u = 2.0 - p2
            r = pltpu.reciprocal(p2 * u, approx=True) * scale[...]
            d = (g[s, rows].astype(f32) - p2) * r
            xd[slot, s] = d.astype(bf16)
            xe[slot, s] = (u * d).astype(bf16)

    def back(n, j, slot):
        zz, yy = chip(n)
        q0, q1, _ = split3(qb[zz, j, yy] * inv_s)
        qq = jnp.concatenate([q0, q1], axis=0)
        share = None
        for s in range(2):
            d = xd[slot, s]
            acc[s, 0] += jnp.dot(qq, d, preferred_element_type=f32)
            acc[s, 1] += jnp.dot(qq, xe[slot, s], preferred_element_type=f32)
            o = lax.dot_general(fw[s], d, (((1,), (1,)), ((), ())), preferred_element_type=f32)
            share = o if share is None else share + o
        part[j, n] = share[:16] + share[16:]

    def sib_send(k):
        pair = pl.ds(2 * k, 2)
        return remote(part.at[1 - c, pair], sib.at[pair], sib_s.at[k], sib_r.at[k], sibling)

    def in_send(n):
        zz, yy = chip(n)
        return remote(part.at[c, n], inbox.at[n], in_s.at[n], in_r.at[n], snp_id(zz, yy, c))

    def reduce_core(k):
        sib_send(k).wait_recv()
        pair = pl.ds(2 * k, 2)
        part[c, pair] = part[c, pair] + sib[pair]

    fwd(0, 1 - c).wait_recv()
    load_g(0).wait()
    front(0, 0, 0)
    front(0, 1, 1)
    back(0, 0, 0)
    pl.semaphore_wait(column, 1)

    @pl.loop(Z, CHIPS)
    def _(n):
        q_out(n).start()

    for n in range(1, 3):
        q_in_from(n).wait_recv()
        fwd(n, c).start()

    @pl.loop(0, Z - 1)
    def _(k):
        q_in_from(2 * k + 3).wait_recv()
        fwd(2 * k + 3, c).start()

        @pl.when(k < Z - 2)
        def _():
            q_in_from(2 * k + 4).wait_recv()
            fwd(2 * k + 4, c).start()

        @pl.when(k >= 1)
        def _():
            sib_send(k - 1).start()

        @pl.when(k >= 2)
        def _():
            reduce_core(k - 2)
            in_send(2 * k - 3).start()

        @pl.when(k >= 3)
        def _():
            in_send(2 * k - 4).start()

        fwd(2 * k + 1, 1 - c).wait_recv()
        fwd(2 * k + 2, 1 - c).wait_recv()

        @pl.when(k < Z // 2)
        def _():
            load_g(2 * k + 1).wait()

        @pl.when(k < Z // 2 - 1)
        def _():
            load_g(2 * k + 2).wait()

        front(2 * k + 1, 0, 0)
        back(2 * k, 1, 1)
        front(2 * k + 1, 1, 1)
        back(2 * k + 1, 0, 0)
        front(2 * k + 2, 0, 0)
        back(2 * k + 1, 1, 1)
        front(2 * k + 2, 1, 1)
        back(2 * k + 2, 0, 0)

    sib_send(Z - 2).start()
    reduce_core(Z - 3)
    in_send(2 * Z - 6).start()
    in_send(2 * Z - 5).start()
    last = CHIPS - 1
    fwd(last, 1 - c).wait_recv()
    front(last, 0, 0)
    back(last - 1, 1, 1)
    front(last, 1, 1)
    back(last, 0, 0)
    back(last, 1, 1)
    sib_send(Z - 1).start()
    reduce_core(Z - 2)
    in_send(2 * Z - 3).start()
    in_send(2 * Z - 4).start()

    counts = jnp.sum(qsum[...], axis=1, keepdims=True)
    for s in range(2):
        diff = (acc[s, 0, :16] + acc[s, 0, 16:]) * (4.0 * inv_c)
        hit = (acc[s, 1, :16] + acc[s, 1, 16:]) * (2.0 * inv_c) + 2.0 * counts
        for rg in range(2):
            for lh in range(2):
                i = s * 4 + rg * 2 + lh
                bsend[i, 0] = hit[rg * 8:rg * 8 + 8, lh * 128:lh * 128 + 128]
                bsend[i, 1] = diff[rg * 8:rg * 8 + 8, lh * 128:lh * 128 + 128]

    def b_copy(da):
        to = lax.rem(a + da, SAMP)
        return remote(bsend.at[to], bin_.at[a], b_s.at[da], b_r.at[a], {"samp": to})

    def b_from(da):
        src = lax.rem(a + da, SAMP)
        return remote(bsend.at[a], bin_.at[src], b_s.at[da], b_r.at[src], {"samp": src})

    def n_copy(da):
        return remote(nfp.at[a], nfp.at[a], n_s.at[da], n_r.at[a], {"samp": lax.rem(a + da, SAMP)})

    def n_from(da):
        src = lax.rem(a + da, SAMP)
        return remote(nfp.at[src], nfp.at[src], n_s.at[da], n_r.at[src], {"samp": src})

    @pl.loop(1, SAMP)
    def _(da):
        b_copy(da).start()

    reduce_core(Z - 1)
    in_send(CHIPS - 1).start()
    in_send(CHIPS - 2).start()

    @pl.loop(1, SAMP)
    def _(da):
        b_from(da).wait_recv()

    bin_[a] = bsend[a]
    both = jnp.sum(bin_[...], axis=0)
    f = fp[a]
    weighted = f * both[0]
    nfp[a] = weighted / (weighted + (1.0 - f) * (both[0] - both[1]))

    @pl.loop(1, SAMP)
    def _(da):
        n_copy(da).start()

    @pl.loop(1, CHIPS)
    def _(n):
        remote(part.at[c, n], inbox.at[n], in_s.at[n], in_r.at[n], sibling).wait_recv()

    inbox[0] = part[c, 0]

    @pl.loop(1, SAMP)
    def _(da):
        n_from(da).wait_recv()

    for s in range(2):
        for rg in range(2):
            for lh in range(2):
                nf_ref[s, rg * 8:rg * 8 + 8, lh * 128:lh * 128 + 128] = nfp[s * 4 + rg * 2 + lh]

    q = qb[z, c, yh]
    share = jnp.sum(inbox[...], axis=0) * (4.0 * inv_s)
    rest = total - jnp.sum(q * share, axis=0, keepdims=True)
    na_ref[...] = q * (share + rest) * (1.0 / total)

    @pl.loop(0, CHIPS)
    def _(n):
        fwd(n, c).wait_send()

    @pl.loop(1, CHIPS)
    def _(n):
        q_out(n).wait_send()
        in_send(n).wait_send()

    @pl.loop(0, Z)
    def _(k):
        sib_send(k).wait_send()

    @pl.loop(1, SAMP)
    def _(da):
        b_copy(da).wait_send()
        n_copy(da).wait_send()


def on_device(genotypes, ancestry, frequencies):
    slabs, rows, cols = genotypes.shape
    k = ancestry.shape[0]
    total = 2.0 * slabs * cols * lax.axis_size("snp")
    dma = pltpu.SemaphoreType.DMA
    vmem = pltpu.VMEM
    return pl.pallas_call(
        functools.partial(kernel, total),
        out_shape=(
            jax.ShapeDtypeStruct(frequencies.shape, f32),
            jax.ShapeDtypeStruct(ancestry.shape, f32),
        ),
        in_specs=[
            pl.BlockSpec(memory_space=pltpu.HBM),
            pl.BlockSpec(memory_space=pltpu.HBM),
            pl.BlockSpec(memory_space=pltpu.HBM),
        ],
        out_specs=(pl.BlockSpec(memory_space=vmem), pl.BlockSpec(memory_space=vmem)),
        scratch_shapes=[
            vmem(genotypes.shape, bf16),
            vmem(frequencies.shape, f32),
            vmem((Z, CORES, YH, k, BLOCK), f32),
            vmem((2, slabs, BLOCK, cols), bf16),
            vmem((2, slabs, BLOCK, cols), bf16),
            vmem((slabs, 2, 2 * k, cols), f32),
            vmem((k, BLOCK), f32),
            vmem((slabs, 6 * k, cols), bf16),
            vmem((slabs, 2 * k, cols), bf16),
            vmem((BLOCK, cols), f32),
            vmem((CORES, CHIPS, k, BLOCK), f32),
            vmem((CHIPS, k, BLOCK), f32),
            vmem((CHIPS, k, BLOCK), f32),
            vmem((SAMP, 2, 8, 128), f32),
            vmem((SAMP, 2, 8, 128), f32),
            vmem((SAMP, 8, 128), f32),
            vmem((SAMP, 8, 128), f32),
            dma((Z,)), dma((2,)),
            dma((CHIPS,)), dma((CHIPS,)),
            dma((CHIPS,)), dma((CHIPS,)),
            dma((Z,)), dma((Z,)),
            dma((CHIPS,)), dma((CHIPS,)),
            dma((SAMP,)), dma((SAMP,)),
            dma((SAMP,)), dma((SAMP,)),
            pltpu.SemaphoreType.REGULAR,
        ],
        compiler_params=pltpu.CompilerParams(
            collective_id=0, has_side_effects=True, vmem_limit_bytes=55168 << 10
        ),
        name="em_step",
    )(genotypes, ancestry, frequencies)


def solution(mesh):
    in_specs = (P(None, "samp", "snp"), P(None, ("samp", "snp")), P(None, None, "snp"))
    out_specs = (P(None, None, "snp"), P(None, ("samp", "snp")))
    return jax.shard_map(
        on_device, mesh=mesh, in_specs=in_specs, out_specs=out_specs, check_vma=False
    )
```

```python
import functools

import jax
import jax.numpy as jnp
from jax import lax
from jax.experimental import pallas as pl
from jax.experimental.pallas import tpu as pltpu
from jax.sharding import PartitionSpec as P

MESH = pl.DeviceIdType.MESH
bf16, f32 = jnp.bfloat16, jnp.float32

Z, YH, CORES, SAMP = 8, 2, 2, 8
CHIPS = Z * YH
BLOCK = 256
PLANE = YH * CORES * BLOCK


def split3(x):
    a = x.astype(bf16)
    r = x - a.astype(f32)
    b = r.astype(bf16)
    return a, b, (r - b.astype(f32)).astype(bf16)


def spread(shape, axis, step):
    t = lax.broadcasted_iota(jnp.int32, shape, axis).astype(f32) * step
    return t - jnp.floor(t)


S_STEP, C_STEP = 0.6180339887, 0.7548776662


def kernel(
    total,
    g_hbm, q_hbm, f_hbm, nf_ref, na_ref,
    g, f_ref, qb, xd, xe, acc, qsum, rp, fw, scale, part, sib, inbox,
    bsend, bin_, fp, nfp,
    g_sem, qf_sem, q_s, q_r, y_s, y_r, fwd_s, fwd_r, sib_s, sib_r,
    in_s, in_r, b_s, b_r, n_s, n_r,
):
    me = lax.axis_index("snp")
    a = lax.axis_index("samp")
    c = lax.rem(me, 2)
    yh = lax.rem(me // 2, 2)
    z = me // 4

    def snp_id(zz, yy, cc):
        return {"snp": zz * 4 + yy * 2 + cc}

    sibling = snp_id(z, yh, 1 - c)

    def plane(k):
        step = ((k + 1) // 2) * (2 * lax.rem(k, 2) - 1)
        return lax.rem(z + step + Z, Z)

    def chip(n):
        return plane(lax.rem(n, Z)), lax.rem(yh + n // Z, 2)

    def remote(src, dst, ss, rs, dev):
        return pltpu.make_async_remote_copy(
            src_ref=src, dst_ref=dst, send_sem=ss, recv_sem=rs,
            device_id=dev, device_id_type=MESH,
        )

    def load_g(k):
        rows = pl.ds(pl.multiple_of(plane(k) * PLANE, PLANE), PLANE)
        return pltpu.make_async_copy(g_hbm.at[:, rows], g.at[:, rows], g_sem.at[k])

    bar = pltpu.get_barrier_semaphore()
    ymate = snp_id(z, 1 - yh, c)
    pl.semaphore_signal(bar, inc=1, device_id=ymate, device_id_type=MESH)
    for n in range(1, Z):
        zz, yy = chip(n)
        pl.semaphore_signal(bar, inc=1, device_id=snp_id(zz, yy, c), device_id_type=MESH)
    pl.semaphore_signal(bar, inc=1, device_id=sibling, device_id_type=MESH)
    for da in range(1, SAMP):
        pl.semaphore_signal(bar, inc=1, device_id={"samp": lax.rem(a + da, SAMP)}, device_id_type=MESH)

    q_in = pltpu.make_async_copy(q_hbm, qb.at[z, c, yh], qf_sem.at[0])
    f_in = pltpu.make_async_copy(f_hbm, f_ref, qf_sem.at[1])
    q_in.start()
    f_in.start()

    @pl.loop(0, Z)
    def _(k):
        load_g(k).start()

    inv_c = jnp.exp2(-spread((1, BLOCK), 1, C_STEP))
    inv_s = jnp.exp2(-spread((1, BLOCK), 1, S_STEP))
    scale[...] = jnp.exp2(spread((BLOCK, BLOCK), 0, S_STEP) + spread((BLOCK, BLOCK), 1, C_STEP))
    f_in.wait()
    for s in range(2):
        f = f_ref[s]
        f0, f1, f2 = split3(2.0 * f)
        rp[s] = jnp.concatenate([f0, f1, f2, f0, f1, f0], axis=0)
        d0, d1, _ = split3(f * inv_c)
        fw[s] = jnp.concatenate([d0, d1], axis=0)
        for rg in range(2):
            for lh in range(2):
                fp[s * 4 + rg * 2 + lh] = f[rg * 8:rg * 8 + 8, lh * 128:lh * 128 + 128]
    acc[...] = jnp.zeros_like(acc)
    qsum[...] = jnp.zeros_like(qsum)
    xd[1] = jnp.zeros(xd.shape[1:], bf16)
    xe[1] = jnp.zeros(xe.shape[1:], bf16)

    q_in.wait()
    pl.semaphore_wait(bar, Z + SAMP)

    def q_out(n):
        step = ((n + 1) // 2) * (2 * lax.rem(n, 2) - 1)
        here = qb.at[z, c, yh]
        return remote(here, here, q_s.at[n], q_r.at[n], snp_id(lax.rem(z - step + Z, Z), yh, c))

    def q_in_from(n):
        here = qb.at[plane(n), c, yh]
        return remote(here, here, q_s.at[n], q_r.at[n], snp_id(plane(n), yh, c))

    def y_out(n):
        here = qb.at[plane(n), c, yh]
        return remote(here, here, y_s.at[n], y_r.at[n], ymate)

    def y_in(n):
        here = qb.at[plane(n), c, 1 - yh]
        return remote(here, here, y_s.at[n], y_r.at[n], ymate)

    def fwd(n, core):
        zz, yy = chip(n)
        here = qb.at[zz, core, yy]
        return remote(here, here, fwd_s.at[n], fwd_r.at[n], sibling)

    fwd(0, c).start()
    y_out(0).start()

    @pl.loop(1, Z)
    def _(n):
        q_out(n).start()

    def front(n, j, slot):
        zz, yy = chip(n)
        q = qb[zz, j, yy]
        q0, q1, q2 = split3(q)
        left = jnp.concatenate([q0, q0, q0, q1, q1, q2], axis=0)
        qsum[...] += q
        rows = pl.ds(pl.multiple_of(zz * PLANE + yy * (2 * BLOCK) + j * BLOCK, BLOCK), BLOCK)
        for s in range(2):
            p2 = lax.dot_general(left, rp[s], (((0,), (0,)), ((), ())), preferred_element_type=f32)
            u = 2.0 - p2
            r = pltpu.reciprocal(p2 * u, approx=True) * scale[...]
            d = (g[s, rows].astype(f32) - p2) * r
            xd[slot, s] = d.astype(bf16)
            xe[slot, s] = (u * d).astype(bf16)

    def back(n, j, slot):
        zz, yy = chip(n)
        q0, q1, _ = split3(qb[zz, j, yy] * inv_s)
        qq = jnp.concatenate([q0, q1], axis=0)
        share = None
        for s in range(2):
            d = xd[slot, s]
            acc[s, 0] += jnp.dot(qq, d, preferred_element_type=f32)
            acc[s, 1] += jnp.dot(qq, xe[slot, s], preferred_element_type=f32)
            o = lax.dot_general(fw[s], d, (((1,), (1,)), ((), ())), preferred_element_type=f32)
            share = o if share is None else share + o
        part[j, n] = share[:16] + share[16:]

    def sib_send(k):
        pair = pl.ds(2 * k, 2)
        return remote(part.at[1 - c, pair], sib.at[pair], sib_s.at[k], sib_r.at[k], sibling)

    def in_send(n):
        zz, yy = chip(n)
        return remote(part.at[c, n], inbox.at[n], in_s.at[n], in_r.at[n], snp_id(zz, yy, c))

    def reduce_core(k):
        sib_send(k).wait_recv()
        pair = pl.ds(2 * k, 2)
        part[c, pair] = part[c, pair] + sib[pair]

    fwd(0, 1 - c).wait_recv()
    load_g(0).wait()
    front(0, 0, 0)
    front(0, 1, 1)
    back(0, 0, 0)

    def pass_on(n):
        q_in_from(n).wait_recv()
        y_out(n).start()
        fwd(n, c).start()

    def y_on(n):
        y_in(n - Z).wait_recv()
        fwd(n, c).start()

    pass_on(1)
    pass_on(2)

    @pl.loop(0, Z - 1)
    def _(k):
        @pl.when(k >= 1)
        def _():
            sib_send(k - 1).start()

        @pl.when(k < 3)
        def _():
            pass_on(2 * k + 3)

        @pl.when(k < 2)
        def _():
            pass_on(2 * k + 4)

        @pl.when(k >= 3)
        def _():
            y_on(2 * k + 3)

        @pl.when(jnp.logical_and(k >= 2, k < Z - 2))
        def _():
            y_on(2 * k + 4)

        @pl.when(k >= 2)
        def _():
            reduce_core(k - 2)
            in_send(2 * k - 3).start()

        @pl.when(k >= 3)
        def _():
            in_send(2 * k - 4).start()

        fwd(2 * k + 1, 1 - c).wait_recv()
        fwd(2 * k + 2, 1 - c).wait_recv()

        @pl.when(k < Z // 2)
        def _():
            load_g(2 * k + 1).wait()

        @pl.when(k < Z // 2 - 1)
        def _():
            load_g(2 * k + 2).wait()

        front(2 * k + 1, 0, 0)
        back(2 * k, 1, 1)
        front(2 * k + 1, 1, 1)
        back(2 * k + 1, 0, 0)
        front(2 * k + 2, 0, 0)
        back(2 * k + 1, 1, 1)
        front(2 * k + 2, 1, 1)
        back(2 * k + 2, 0, 0)

    sib_send(Z - 2).start()
    reduce_core(Z - 3)
    in_send(2 * Z - 6).start()
    in_send(2 * Z - 5).start()
    last = CHIPS - 1
    fwd(last, 1 - c).wait_recv()
    front(last, 0, 0)
    back(last - 1, 1, 1)
    front(last, 1, 1)
    back(last, 0, 0)
    back(last, 1, 1)
    sib_send(Z - 1).start()
    reduce_core(Z - 2)
    in_send(2 * Z - 3).start()
    in_send(2 * Z - 4).start()

    counts = jnp.sum(qsum[...], axis=1, keepdims=True)
    for s in range(2):
        diff = (acc[s, 0, :16] + acc[s, 0, 16:]) * (4.0 * inv_c)
        hit = (acc[s, 1, :16] + acc[s, 1, 16:]) * (2.0 * inv_c) + 2.0 * counts
        for rg in range(2):
            for lh in range(2):
                i = s * 4 + rg * 2 + lh
                bsend[i, 0] = hit[rg * 8:rg * 8 + 8, lh * 128:lh * 128 + 128]
                bsend[i, 1] = diff[rg * 8:rg * 8 + 8, lh * 128:lh * 128 + 128]

    def b_copy(da):
        to = lax.rem(a + da, SAMP)
        return remote(bsend.at[to], bin_.at[a], b_s.at[da], b_r.at[a], {"samp": to})

    def b_from(da):
        src = lax.rem(a + da, SAMP)
        return remote(bsend.at[a], bin_.at[src], b_s.at[da], b_r.at[src], {"samp": src})

    def n_copy(da):
        return remote(nfp.at[a], nfp.at[a], n_s.at[da], n_r.at[a], {"samp": lax.rem(a + da, SAMP)})

    def n_from(da):
        src = lax.rem(a + da, SAMP)
        return remote(nfp.at[src], nfp.at[src], n_s.at[da], n_r.at[src], {"samp": src})

    @pl.loop(1, SAMP)
    def _(da):
        b_copy(da).start()

    reduce_core(Z - 1)
    in_send(CHIPS - 1).start()
    in_send(CHIPS - 2).start()

    @pl.loop(1, SAMP)
    def _(da):
        b_from(da).wait_recv()

    bin_[a] = bsend[a]
    both = jnp.sum(bin_[...], axis=0)
    f = fp[a]
    weighted = f * both[0]
    nfp[a] = weighted / (weighted + (1.0 - f) * (both[0] - both[1]))

    @pl.loop(1, SAMP)
    def _(da):
        n_copy(da).start()

    @pl.loop(1, CHIPS)
    def _(n):
        remote(part.at[c, n], inbox.at[n], in_s.at[n], in_r.at[n], sibling).wait_recv()

    inbox[0] = part[c, 0]

    @pl.loop(1, SAMP)
    def _(da):
        n_from(da).wait_recv()

    for s in range(2):
        for rg in range(2):
            for lh in range(2):
                nf_ref[s, rg * 8:rg * 8 + 8, lh * 128:lh * 128 + 128] = nfp[s * 4 + rg * 2 + lh]

    q = qb[z, c, yh]
    share = jnp.sum(inbox[...], axis=0) * (4.0 * inv_s)
    rest = total - jnp.sum(q * share, axis=0, keepdims=True)
    na_ref[...] = q * (share + rest) * (1.0 / total)

    @pl.loop(0, CHIPS)
    def _(n):
        fwd(n, c).wait_send()

    y_out(0).wait_send()

    @pl.loop(1, Z)
    def _(n):
        q_out(n).wait_send()
        y_out(n).wait_send()

    @pl.loop(1, CHIPS)
    def _(n):
        in_send(n).wait_send()

    @pl.loop(0, Z)
    def _(k):
        sib_send(k).wait_send()

    @pl.loop(1, SAMP)
    def _(da):
        b_copy(da).wait_send()
        n_copy(da).wait_send()


def on_device(genotypes, ancestry, frequencies):
    slabs, rows, cols = genotypes.shape
    k = ancestry.shape[0]
    total = 2.0 * slabs * cols * lax.axis_size("snp")
    dma = pltpu.SemaphoreType.DMA
    vmem = pltpu.VMEM
    return pl.pallas_call(
        functools.partial(kernel, total),
        out_shape=(
            jax.ShapeDtypeStruct(frequencies.shape, f32),
            jax.ShapeDtypeStruct(ancestry.shape, f32),
        ),
        in_specs=[
            pl.BlockSpec(memory_space=pltpu.HBM),
            pl.BlockSpec(memory_space=pltpu.HBM),
            pl.BlockSpec(memory_space=pltpu.HBM),
        ],
        out_specs=(pl.BlockSpec(memory_space=vmem), pl.BlockSpec(memory_space=vmem)),
        scratch_shapes=[
            vmem(genotypes.shape, bf16),
            vmem(frequencies.shape, f32),
            vmem((Z, CORES, YH, k, BLOCK), f32),
            vmem((2, slabs, BLOCK, cols), bf16),
            vmem((2, slabs, BLOCK, cols), bf16),
            vmem((slabs, 2, 2 * k, cols), f32),
            vmem((k, BLOCK), f32),
            vmem((slabs, 6 * k, cols), bf16),
            vmem((slabs, 2 * k, cols), bf16),
            vmem((BLOCK, cols), f32),
            vmem((CORES, CHIPS, k, BLOCK), f32),
            vmem((CHIPS, k, BLOCK), f32),
            vmem((CHIPS, k, BLOCK), f32),
            vmem((SAMP, 2, 8, 128), f32),
            vmem((SAMP, 2, 8, 128), f32),
            vmem((SAMP, 8, 128), f32),
            vmem((SAMP, 8, 128), f32),
            dma((Z,)), dma((2,)),
            dma((Z,)), dma((Z,)),
            dma((Z,)), dma((Z,)),
            dma((CHIPS,)), dma((CHIPS,)),
            dma((Z,)), dma((Z,)),
            dma((CHIPS,)), dma((CHIPS,)),
            dma((SAMP,)), dma((SAMP,)),
            dma((SAMP,)), dma((SAMP,)),
        ],
        compiler_params=pltpu.CompilerParams(
            collective_id=0, has_side_effects=True, vmem_limit_bytes=55168 << 10
        ),
        name="em_step",
    )(genotypes, ancestry, frequencies)


def solution(mesh):
    in_specs = (P(None, "samp", "snp"), P(None, ("samp", "snp")), P(None, None, "snp"))
    out_specs = (P(None, None, "snp"), P(None, ("samp", "snp")))
    return jax.shard_map(
        on_device, mesh=mesh, in_specs=in_specs, out_specs=out_specs, check_vma=False
    )
```
